512 devices in a mesh: fsdp: 64 (over x_hi, z, core), seq: 8 (over x_lo, y).
Axes of the slice: x: 4 (x_hi: 2, x_lo: 2; x = x_hi * 2 + x_lo), y: 4, z: 16, core: 2. Of those that a mesh axis runs over, the one named last changes fastest.
Arguments:
- attended: bfloat16 [64, 2, 1024, 1536], P('fsdp', None, 'seq'), may hold values from -6 to 6
- residual: bfloat16 [64, 2, 1024, 3072], P('fsdp', None, 'seq'), may hold values from -6 to 6
- targets: bfloat16 [64, 2, 1024, 64], P('fsdp', None, 'seq'), may hold values from -6 to 6
- repaint_mask: int32 [64, 1024], P('fsdp', 'seq'), may hold values from 0 to 1, as said below
- timesteps: int32 [64], P('fsdp'), may hold values from 0 to 999
- modulation: float32 [64, 3, 3072], P('fsdp'), may hold values from -4 to 4
- output_weight: bfloat16 [1536, 3072], P('fsdp'), may hold values from -0.15625 to 0.15625
- adapter_down: bfloat16 [1536, 128], P('fsdp'), may hold values from -0.15625 to 0.15625
- adapter_up: bfloat16 [3072, 128], P('fsdp'), may hold values from -0.15625 to 0.15625
- latent_weight: bfloat16 [3072, 64], P('fsdp'), may hold values from -0.109375 to 0.109375
Outputs:
- pair_loss: float32 [64], P('fsdp')
- grad_down: float32 [1536, 128], P('fsdp')
- up_gradient: float32 [3072, 128], P('fsdp')
The draws below stay inside these ranges and needn't reach their ends.
Inputs may be any that keep to these rules, and one draw needn't show every extreme that they name: `repaint_mask`: 1 marks an image token to be repainted; a pair's winner and loser share the mask.
All inputs are finite; a program needn't handle non-finite values.
Results may differ from the reference program's by a relative error of at most 0.0065.
Values may be sent and summed in bfloat16 or wider, within the bound.
No kernel may reach another device: no remote copies, remote signals or barrier semaphores. Data moves between devices by JAX's collectives and lax.ppermute only.
A program may use at most 64 MiB of HBM per device.

```python
import jax
import jax.numpy as jnp
from jax import lax

MODEL_FEATURES = 3072
C = 64
HALF_HEAD_WIDTH = 1536
ADAPTER_RANK = 128
PAIRS = 64
IMG = 1024


def draw_repaint_mask(key, part):
    key = jax.random.fold_in(key, 11)
    samples = jax.random.randint(key, (PAIRS, IMG), 0, 1000)
    threshold = 150 + 450 * jnp.arange(IMG, dtype=jnp.int32) // IMG
    return (samples < threshold[None, :]).astype(jnp.int32)


def touch_ends(result, key, least, largest):
    longest = result.shape.index(max(result.shape))
    spots = []
    for shift in (0, 1):
        where = [jax.random.randint(jax.random.fold_in(key, axis), (), 0, length) for axis, length in enumerate(result.shape)]
        where[longest] = (where[longest] + shift) % result.shape[longest]
        spots.append(tuple(where))
    return result.at[spots[0]].set(least).at[spots[1]].set(largest)


def shard_levels(key, extent, pieces, least, top_value):
    def one(dim, blocks):
        steps = jax.random.uniform(jax.random.fold_in(jax.random.fold_in(key, 6), dim), (blocks,), jnp.float32, least / len(pieces), top_value / len(pieces))
        return jnp.repeat(jnp.exp(steps), extent[dim] // blocks).reshape((-1,) + (1,) * (len(extent) - dim - 1))

    level = one(*pieces[0])
    for cut in pieces[1:]:
        level = level * one(*cut)
    return level


def noise(stream_key, shape, scale, most, split=(), kind=jnp.bfloat16):
    entries = jax.random.normal(stream_key, shape, jnp.float32) * scale
    if len(split) > 0:
        entries = shard_levels(stream_key, shape, split, -0.22, 0.18) * entries
    return jnp.clip(entries, min=-most, max=most).astype(kind)


def setup_inputs(seed: int = 0) -> dict:
    splits = jax.random.split(jax.random.key(seed), 11)
    attended = noise(splits[0], (PAIRS, 2, IMG, HALF_HEAD_WIDTH), 1.0, 6.0, ((0, 64), (2, 8)))
    residual = noise(splits[1], (PAIRS, 2, IMG, MODEL_FEATURES), 1.0, 6.0, ((0, 64), (2, 8)))
    targets = noise(splits[2], (PAIRS, 2, IMG, C), 1.0, 6.0, ((0, 64), (2, 8)))
    repaint_mask = draw_repaint_mask(jax.random.fold_in(splits[10], 71), 0)
    timesteps = touch_ends(jax.random.randint(splits[4], (PAIRS,), 0, 1000), jax.random.fold_in(splits[4], 1), 0, 999).astype(jnp.int32)
    modulation = noise(splits[5], (PAIRS, 3, MODEL_FEATURES), 0.5, 4.0, ((0, 64),), jnp.float32)
    output_weight = noise(splits[6], (HALF_HEAD_WIDTH, MODEL_FEATURES), HALF_HEAD_WIDTH ** -0.5, 0.15625, ((0, 64),))
    adapter_down = noise(splits[7], (HALF_HEAD_WIDTH, ADAPTER_RANK), HALF_HEAD_WIDTH ** -0.5, 0.15625, ((0, 64),))
    adapter_up = noise(splits[8], (MODEL_FEATURES, ADAPTER_RANK), (11 * ADAPTER_RANK) ** -0.5, 0.15625, ((0, 64),))
    latent_weight = noise(splits[9], (MODEL_FEATURES, C), MODEL_FEATURES ** -0.5, 0.109375, ((0, 64),))
    return dict(attended=attended, residual=residual, targets=targets, repaint_mask=repaint_mask, timesteps=timesteps, modulation=modulation, output_weight=output_weight, adapter_down=adapter_down, adapter_up=adapter_up, latent_weight=latent_weight)


NORM_EPS = 1e-06
DPO_BETA = 10.0
ADAPTER_SCALE = 1.0

def layer_norm(hidden):
    centred = hidden - lax.optimization_barrier(jnp.mean(hidden, axis=-1, keepdims=True))
    inverse = lax.rsqrt(lax.optimization_barrier(jnp.mean(centred * centred, axis=-1, keepdims=True)) + NORM_EPS)
    return (centred * inverse, inverse)

def head_out(stream, update, gate_term, scale_term, shift_term, latent_weight):
    hidden = stream.astype(jnp.float32) + gate_term * update
    normed, inverse = layer_norm(hidden)
    modulated = (normed * (1.0 + scale_term) + shift_term).astype(jnp.bfloat16)
    flat_rows = modulated.reshape(-1, modulated.shape[-1])
    predicted = jnp.dot(flat_rows, latent_weight, preferred_element_type=jnp.float32)
    return (predicted.reshape(modulated.shape[:-1] + (latent_weight.shape[1],)), normed, inverse)

def head_back(grad_pred, normed, inverse, gate_term, scale_term, latent_weight):
    flat_grad = grad_pred.reshape(-1, grad_pred.shape[-1])
    grad_mod = lax.dot_general(flat_grad, latent_weight, (((1,), (1,)), ((), ())), preferred_element_type=jnp.float32)
    grad_norm = grad_mod.reshape(normed.shape) * (1.0 + scale_term)
    centred = grad_norm - lax.optimization_barrier(jnp.mean(grad_norm, axis=-1, keepdims=True))
    grad_hidden = inverse * (centred - normed * lax.optimization_barrier(jnp.mean(grad_norm * normed, axis=-1, keepdims=True)))
    return (gate_term * grad_hidden).astype(jnp.bfloat16)

def reference(attended, residual, targets, repaint_mask, timesteps, modulation, output_weight, adapter_down, adapter_up, latent_weight):
    normaliser = float(IMG * C)

    def one_pair(carry, inputs):
        attn_pair, res_pair, target_pair, mask_pair, step_pair, mod_pair = inputs
        shift_term = mod_pair[0]
        scale_term = mod_pair[1]
        gate_term = mod_pair[2]
        mask_col = mask_pair.astype(jnp.float32)[:, None]
        errors_pol = []
        errors_ref = []
        stored = []
        for kind in range(2):
            attention_rows = attn_pair[kind]
            frozen_output = jnp.dot(attention_rows, output_weight, preferred_element_type=jnp.float32)
            down_projected = jnp.dot(attention_rows, adapter_down, preferred_element_type=jnp.float32).astype(jnp.bfloat16)
            adapter_term = lax.dot_general(down_projected, adapter_up, (((1,), (1,)), ((), ())), preferred_element_type=jnp.float32)
            policy_model = frozen_output + ADAPTER_SCALE * adapter_term
            pred_pol, normed, inverse = head_out(res_pair[kind], policy_model, gate_term, scale_term, shift_term, latent_weight)
            pred_ref, unused_normed, unused_inverse = head_out(res_pair[kind], frozen_output, gate_term, scale_term, shift_term, latent_weight)
            target_rows = target_pair[kind].astype(jnp.float32)
            miss_pol = pred_pol - target_rows
            miss_ref = pred_ref - target_rows
            errors_pol.append(jnp.sum(mask_col * miss_pol * miss_pol) / normaliser)
            errors_ref.append(jnp.sum(mask_col * miss_ref * miss_ref) / normaliser)
            stored.append((attention_rows, down_projected, miss_pol, normed, inverse))
        delta = errors_pol[0] - errors_ref[0] - (errors_pol[1] - errors_ref[1])
        weight_t = 2.0 - step_pair.astype(jnp.float32) / 1000.0
        logits = -DPO_BETA * weight_t * delta
        pair_loss = jax.nn.softplus(-logits)
        slope = jax.nn.sigmoid(-logits) * DPO_BETA * weight_t / normaliser
        grad_down, up_gradient = carry
        for kind in range(2):
            attention_rows, down_projected, miss_pol, normed, inverse = stored[kind]
            weighting = slope * (1.0 - 2.0 * kind)
            grad_pred = (weighting * 2.0 * mask_col * miss_pol).astype(jnp.bfloat16)
            gradient_delta = head_back(grad_pred, normed, inverse, gate_term, scale_term, latent_weight)
            up_gradient = up_gradient + ADAPTER_SCALE * jnp.dot(gradient_delta.T, down_projected, preferred_element_type=jnp.float32)
            gradient_lowrank = (ADAPTER_SCALE * jnp.dot(gradient_delta, adapter_up, preferred_element_type=jnp.float32)).astype(jnp.bfloat16)
            grad_down = grad_down + jnp.dot(attention_rows.T, gradient_lowrank, preferred_element_type=jnp.float32)
        return ((grad_down, up_gradient), pair_loss)
    start = (jnp.zeros((HALF_HEAD_WIDTH, ADAPTER_RANK), jnp.float32), jnp.zeros((MODEL_FEATURES, ADAPTER_RANK), jnp.float32))
    sums, pair_loss = lax.scan(one_pair, start, (attended, residual, targets, repaint_mask, timesteps, modulation))
    return (pair_loss, sums[0], sums[1])
```

```python
import jax
import jax.numpy as jnp
from jax import lax
from jax.sharding import Mesh
from jax.sharding import PartitionSpec as P

NORM_EPS = 1e-06
DPO_BETA = 10.0
ADAPTER_SCALE = 1.0
FINE = ("xh", "z", "c", "xl", "y")
OWNERS = ("xh", "z", "c")
TOKENS = ("xl", "y")
LANES = 128


def layer_norm(hidden):
    centred = hidden - jnp.mean(hidden, axis=-1, keepdims=True)
    inverse = lax.rsqrt(jnp.mean(centred * centred, axis=-1, keepdims=True) + NORM_EPS)
    return (centred * inverse, inverse)


def head_out(stream, update, gate_term, scale_term, shift_term, latent_weight):
    hidden = stream.astype(jnp.float32) + gate_term * update
    normed, inverse = layer_norm(hidden)
    modulated = (normed * (1.0 + scale_term) + shift_term).astype(jnp.bfloat16)
    predicted = jnp.dot(modulated, latent_weight, preferred_element_type=jnp.float32)
    return (predicted, normed, inverse)


def head_back(grad_pred, normed, inverse, gate_term, scale_term, latent_weight):
    grad_mod = lax.dot_general(
        grad_pred, latent_weight, (((1,), (1,)), ((), ())), preferred_element_type=jnp.float32
    )
    grad_norm = grad_mod * (1.0 + scale_term)
    centred = grad_norm - jnp.mean(grad_norm, axis=-1, keepdims=True)
    grad_hidden = inverse * (
        centred - normed * jnp.mean(grad_norm * normed, axis=-1, keepdims=True)
    )
    return (gate_term * grad_hidden).astype(jnp.bfloat16)


def spread(value, axes, size):
    return lax.all_to_all(jnp.broadcast_to(value[None], (size,) + value.shape), axes, 0, 0)


def by_core(core, here, there):
    first = jnp.where(core == 0, here, there)
    second = jnp.where(core == 0, there, here)
    return first, second


def local(
    attended,
    residual,
    targets,
    repaint_mask,
    timesteps,
    modulation,
    output_weight,
    adapter_down,
    adapter_up,
    latent_weight,
):
    _, kinds, tokens, head_width = attended.shape
    width = residual.shape[-1]
    channels = targets.shape[-1]
    rank = adapter_down.shape[1]
    rows = kinds * tokens
    own = output_weight.shape[0]
    half = width // 2
    xs, zs = lax.axis_size("xh"), lax.axis_size("z")
    seqs = lax.axis_size("xl") * lax.axis_size("y")
    core = lax.axis_index("c")
    swap = [(0, 1), (1, 0)]

    packed = jnp.stack(
        [
            jnp.concatenate([output_weight[:, :half], adapter_down, adapter_up[:own]], axis=1),
            jnp.concatenate(
                [output_weight[:, half:], adapter_up[own:], latent_weight[:own], latent_weight[own:]],
                axis=1,
            ),
        ]
    )
    packed = jnp.broadcast_to(packed[None], (xs,) + packed.shape).reshape(
        (xs * 2,) + packed.shape[1:]
    )
    packed = lax.all_to_all(packed, ("xh", "c"), 0, 0)
    here = lax.all_gather(packed, "z", axis=0)
    here = here.reshape(head_width, -1)
    there = lax.ppermute(here, "c", swap)

    flat_in = attended.reshape(rows, head_width)
    flat_in = (
        flat_in.reshape(rows, xs, zs, -1).transpose(0, 2, 1, 3).reshape(rows, head_width)
    )
    stream = residual.reshape(rows, width)
    stream = jnp.where(core == 0, stream, jnp.roll(stream, half, axis=1))
    terms = modulation[0]
    terms = jnp.where(core == 0, terms, jnp.roll(terms, half, axis=1))
    shift_term, scale_term, gate_term = terms[0:1], terms[1:2], terms[2:3]

    out_here = jnp.dot(flat_in, here, preferred_element_type=jnp.float32)
    out_there = jnp.dot(flat_in, there, preferred_element_type=jnp.float32)
    frozen_output = jnp.concatenate([out_here[:, :half], out_there[:, :half]], axis=1)
    down_projected = jnp.where(
        core == 0, out_here[:, half : half + rank], out_there[:, half : half + rank]
    ).astype(jnp.bfloat16)

    small0, small1 = by_core(core, here[:, half:], there[:, half:])
    up_parts = jnp.stack([small0[:, rank:], small1[:, :rank]], axis=1)
    last_parts = small1[:, rank:].reshape(head_width, 2, channels)

    def features(parts):
        parts = parts.reshape(zs, xs, 2, own, 2, -1).transpose(1, 0, 2, 4, 3, 5)
        parts = parts.reshape(xs, half, -1)
        parts = jnp.where(core == 0, parts, parts[::-1])
        return parts.reshape(width, -1)

    up_all = features(up_parts)
    final_all = features(last_parts)

    adapter_term = lax.dot_general(
        down_projected, up_all, (((1,), (1,)), ((), ())), preferred_element_type=jnp.float32
    )
    policy_model = frozen_output + ADAPTER_SCALE * adapter_term
    pred_pol, normed, inverse = head_out(
        stream, policy_model, gate_term, scale_term, shift_term, final_all
    )
    pred_ref, _, _ = head_out(stream, frozen_output, gate_term, scale_term, shift_term, final_all)
    mask_rows = jnp.broadcast_to(
        repaint_mask.astype(jnp.float32)[0, None, :, None], (kinds, tokens, 1)
    ).reshape(rows, 1)
    target_rows = targets.reshape(rows, channels).astype(jnp.float32)
    miss_pol = pred_pol - target_rows
    miss_ref = pred_ref - target_rows
    normaliser = float(tokens * seqs * channels)

    def by_kind(value):
        return jnp.sum(value.reshape(kinds, -1), axis=1)

    errors = jnp.concatenate(
        [by_kind(mask_rows * miss_pol * miss_pol), by_kind(mask_rows * miss_ref * miss_ref)]
    )
    errors = jnp.pad((errors / normaliser)[None, :], ((0, 7), (0, LANES - 2 * kinds)))
    summed = jnp.sum(spread(errors, TOKENS, seqs)[:, 0], axis=0)
    delta = summed[0] - summed[2] - (summed[1] - summed[3])
    weight_t = 2.0 - timesteps.astype(jnp.float32) / 1000.0
    logits = -DPO_BETA * weight_t * delta
    pair_loss = jax.nn.softplus(-logits)
    slope = jax.nn.sigmoid(-logits) * DPO_BETA * weight_t / normaliser
    signs = jnp.repeat(jnp.array([1.0, -1.0], jnp.float32), tokens)[:, None]
    grad_pred = (slope * signs * 2.0 * mask_rows * miss_pol).astype(jnp.bfloat16)
    gradient_delta = head_back(grad_pred, normed, inverse, gate_term, scale_term, final_all)
    up_gradient = ADAPTER_SCALE * lax.dot_general(
        gradient_delta, down_projected, (((0,), (0,)), ((), ())), preferred_element_type=jnp.float32
    )
    gradient_lowrank = (
        ADAPTER_SCALE * jnp.dot(gradient_delta, up_all, preferred_element_type=jnp.float32)
    ).astype(jnp.bfloat16)
    grad_down = lax.dot_general(
        flat_in, gradient_lowrank, (((0,), (0,)), ((), ())), preferred_element_type=jnp.float32
    )

    up_gradient = up_gradient.astype(jnp.bfloat16).reshape(xs, zs, 2, 2 * own, rank)
    up_gradient = jnp.where(core == 0, up_gradient, up_gradient[::-1])
    grad_down = grad_down.astype(jnp.bfloat16).reshape(zs, xs, 2, own, rank).transpose(1, 0, 2, 3, 4)
    grads = jnp.concatenate([grad_down, up_gradient], axis=3)
    grads = grads.reshape(xs * zs, 2, 3 * own, rank)
    mine, other = by_core(core, grads[:, 0], grads[:, 1])
    mine = mine.astype(jnp.float32) + lax.ppermute(other, "c", swap).astype(jnp.float32)
    piece = 3 * own // seqs
    mine = mine.astype(jnp.bfloat16).reshape(xs * zs, seqs, piece, rank).transpose(1, 0, 2, 3)
    mine = lax.all_to_all(mine, TOKENS, 0, 0)
    mine = jnp.sum(mine.astype(jnp.float32), axis=0).astype(jnp.bfloat16)
    mine = lax.all_to_all(mine, ("xh", "z"), 0, 0)
    mine = jnp.sum(mine.astype(jnp.float32), axis=0)
    mine = spread(mine, TOKENS, seqs).reshape(3 * own, rank)
    return (pair_loss, mine[:own], mine[own:])


def solution(mesh):
    seqs = mesh.shape["seq"]
    fsdp = mesh.shape["fsdp"]
    fine = Mesh(mesh.devices.reshape(2, fsdp // 4, 2, 2, seqs // 2), FINE)
    in_specs = (
        P(OWNERS, None, TOKENS, None),
        P(OWNERS, None, TOKENS, None),
        P(OWNERS, None, TOKENS, None),
        P(OWNERS, TOKENS),
        P(OWNERS),
        P(OWNERS, None, None),
        P(OWNERS, None),
        P(OWNERS, None),
        P(OWNERS, None),
        P(OWNERS, None),
    )
    out_specs = (P(OWNERS), P(OWNERS, None), P(OWNERS, None))
    return jax.shard_map(local, mesh=fine, in_specs=in_specs, out_specs=out_specs, check_vma=False)
```

```python
import jax
import jax.numpy as jnp
from jax import lax
from jax.sharding import Mesh
from jax.sharding import PartitionSpec as P

NORM_EPS = 1e-06
DPO_BETA = 10.0
ADAPTER_SCALE = 1.0
FINE = ("xh", "z", "c", "xl", "y")
OWNERS = ("xh", "z", "c")
TOKENS = ("xl", "y")
F32 = jnp.float32
BF16 = jnp.bfloat16
SWAP = [(0, 1), (1, 0)]


def exact_dot(a, b):
    return jnp.dot(a, b, preferred_element_type=F32, precision=lax.Precision.HIGHEST)


def dot(a, b):
    return jnp.dot(a, b, preferred_element_type=F32)


def dot_t(a, b):
    return lax.dot_general(a, b, (((1,), (1,)), ((), ())), preferred_element_type=F32)


def t_dot(a, b):
    return lax.dot_general(a, b, (((0,), (0,)), ((), ())), preferred_element_type=F32)


def spread(value, axes, size):
    return lax.all_to_all(jnp.broadcast_to(value[None], (size,) + value.shape), axes, 0, 0)


def gather_small(down, up, last, zs, seqs, core, seq):
    own, rank = down.shape
    channels = last.shape[1]
    packed = jnp.concatenate(
        [down, up, jnp.concatenate([last[:own], last[own:]], axis=1)], axis=0
    )
    piece = 4 * own // (2 * seqs)
    packed = packed.reshape(2, seqs, piece, rank)
    packed = lax.dynamic_index_in_dim(packed, seq, 1, keepdims=False)
    packed = jnp.broadcast_to(packed[None], (2 * zs,) + packed.shape)
    packed = lax.all_to_all(packed.reshape((4 * zs, piece, rank)), OWNERS, 0, 0)
    here = spread(packed, TOKENS, seqs)
    there = lax.ppermute(here, "c", SWAP)
    both = jnp.where(core == 0, jnp.stack([here, there]), jnp.stack([there, here]))
    both = both.reshape(2 * seqs, 4 * zs, piece, rank).transpose(1, 0, 2, 3)
    both = both.reshape(4 * zs, 4 * own, rank)
    down = both[:, :own].reshape(-1, rank)
    up = both[:, own : 3 * own].reshape(-1, rank)
    last = both[:, 3 * own :].reshape(4 * zs, own, 2, channels).transpose(0, 2, 1, 3)
    return down, up, last.reshape(-1, channels)


def local(
    attended,
    residual,
    targets,
    repaint_mask,
    timesteps,
    modulation,
    output_weight,
    adapter_down,
    adapter_up,
    latent_weight,
):
    _, kinds, tokens, depth = attended.shape
    width = residual.shape[-1]
    channels = targets.shape[-1]
    rank = adapter_down.shape[1]
    rows = kinds * tokens
    own = output_weight.shape[0]
    zs, ys = lax.axis_size("z"), lax.axis_size("y")
    seqs = 2 * ys
    xh, core = lax.axis_index("xh"), lax.axis_index("c")
    normaliser = float(tokens * seqs * channels)

    pair = lax.ppermute(output_weight, "xh", SWAP)
    pair = jnp.where(
        xh == 0, jnp.stack([output_weight, pair]), jnp.stack([pair, output_weight])
    )
    here = lax.all_gather(pair, "z", axis=0).reshape(depth // 2, width)

    down_all, up_all, final_all = gather_small(
        adapter_down, adapter_up, latent_weight, zs, seqs, core, lax.axis_index(TOKENS)
    )
    flat_in = attended.reshape(rows, depth)
    in_cores = flat_in.reshape(rows, 2, zs, 2, own).transpose(3, 0, 2, 1, 4)
    in_cores = in_cores.reshape(2, rows, depth // 2)
    in_here = jnp.where(core == 0, in_cores[0], in_cores[1])
    in_there = jnp.where(core == 0, in_cores[1], in_cores[0])
    stream = residual.reshape(rows, width).astype(F32)
    shift, scale, gate = modulation[0, 0:1], 1.0 + modulation[0, 1:2], modulation[0, 2:3]
    final32 = final_all.astype(F32)
    scale_final, shift_final = exact_dot(scale, final32), exact_dot(shift, final32)
    down_projected = dot(flat_in, down_all).astype(BF16)
    adapter_term = ADAPTER_SCALE * dot_t(down_projected, up_all)

    here, in_here, in_there, final_all, up_all, down_projected, adapter_term = (
        lax.optimization_barrier(
            (here, in_here, in_there, final_all, up_all, down_projected, adapter_term)
        )
    )
    there = lax.ppermute(here, "c", SWAP)
    frozen = dot(in_here, here) + dot(in_there, there)
    hidden_ref = stream + gate * frozen
    hidden_pol = hidden_ref + gate * adapter_term

    def head_out(hidden):
        centred = hidden - jnp.mean(hidden, axis=-1, keepdims=True)
        variance = jnp.mean(centred * centred, axis=-1, keepdims=True)
        inverse = lax.rsqrt(variance + NORM_EPS)
        normed = centred * inverse
        return dot((normed * scale + shift).astype(BF16), final_all), normed, inverse

    pred_pol, normed, inverse = head_out(hidden_pol)
    pred_ref, _, _ = head_out(hidden_ref)
    target_rows = targets.reshape(rows, channels).astype(F32)
    miss_pol = pred_pol - target_rows
    miss_ref = pred_ref - target_rows
    mask_rows = jnp.broadcast_to(repaint_mask.astype(F32)[0], (kinds, tokens)).reshape(rows, 1)

    def by_kind(value):
        return jnp.sum(value.reshape(kinds, -1), axis=1)

    errors = jnp.concatenate(
        [by_kind(mask_rows * miss_pol * miss_pol), by_kind(mask_rows * miss_ref * miss_ref)]
    )
    weight_t = (2.0 - timesteps.astype(F32) / 1000.0) / seqs
    errors = jnp.concatenate([errors / normaliser, weight_t])
    errors = jnp.pad(errors[None, :], ((0, 7), (0, 127 - 2 * kinds)))
    errors, miss_pol = lax.optimization_barrier((errors, miss_pol))
    errors = spread(errors, ("c",) + TOKENS, 2 * seqs)[:, 0]
    errors = jnp.sum(errors.reshape(2, seqs, 128), axis=1)
    delta = errors[:, 0] - errors[:, 2] - (errors[:, 1] - errors[:, 3])
    weight_t = errors[:, 4]
    logits = -DPO_BETA * weight_t * delta
    pair_loss = lax.dynamic_slice_in_dim(jax.nn.softplus(-logits), core, 1)
    slope = jax.nn.sigmoid(-logits) * DPO_BETA * weight_t / normaliser
    slope_here = jnp.where(core == 0, slope[0], slope[1])
    slope_there = jnp.where(core == 0, slope[1], slope[0])

    signs = jnp.repeat(jnp.array([2.0, -2.0], F32), tokens)[:, None]
    grad_pred = (signs * mask_rows * miss_pol).astype(BF16)
    grad32 = grad_pred.astype(F32)
    first = jnp.sum(grad32 * scale_final, axis=1, keepdims=True) / width
    second = jnp.sum(grad32 * (pred_pol - shift_final), axis=1, keepdims=True) / width
    grad_norm = dot_t(grad_pred, final_all) * scale
    update = (gate * (inverse * (grad_norm - first - normed * second))).astype(BF16)
    up_gradient = ADAPTER_SCALE * t_dot(update, down_projected)
    grad_low = (ADAPTER_SCALE * dot(update, up_all)).astype(BF16)
    down_here = t_dot(in_here, grad_low)
    down_there = t_dot(in_there, grad_low)

    up_gradient = up_gradient.reshape(2, zs, 2, 2 * own, rank)
    up_here = jnp.where(core == 0, up_gradient[:, :, 0], up_gradient[:, :, 1])
    up_there = jnp.where(core == 0, up_gradient[:, :, 1], up_gradient[:, :, 0])

    def by_owner(down, up):
        down = down.reshape(zs, 2, own, rank).transpose(1, 0, 2, 3)
        return jnp.concatenate([down, up], axis=2)

    grads = by_owner(down_there, up_there).astype(BF16)
    grads = lax.ppermute(grads, "c", SWAP).astype(F32)
    grads = slope_here * by_owner(down_here, up_here) + slope_there * grads
    piece = 3 * own // seqs
    grads = grads.astype(BF16).reshape(2, zs, seqs, piece, rank).transpose(0, 2, 1, 3, 4)
    grads = lax.all_to_all(grads.reshape(2 * seqs, zs, piece, rank), ("xh",) + TOKENS, 0, 0)
    grads = jnp.sum(grads.astype(F32), axis=0).astype(BF16)
    grads = jnp.sum(lax.all_to_all(grads, "z", 0, 0).astype(F32), axis=0)
    grads = spread(grads, TOKENS, seqs).reshape(3 * own, rank)
    return (pair_loss, grads[:own], grads[own:])


def solution(mesh):
    seqs = mesh.shape["seq"]
    fsdp = mesh.shape["fsdp"]
    fine = Mesh(mesh.devices.reshape(2, fsdp // 4, 2, 2, seqs // 2), FINE)
    in_specs = (
        P(OWNERS, None, TOKENS, None),
        P(OWNERS, None, TOKENS, None),
        P(OWNERS, None, TOKENS, None),
        P(OWNERS, TOKENS),
        P(OWNERS),
        P(OWNERS, None, None),
        P(OWNERS, None),
        P(OWNERS, None),
        P(OWNERS, None),
        P(OWNERS, None),
    )
    out_specs = (P(OWNERS), P(OWNERS, None), P(OWNERS, None))
    return jax.shard_map(local, mesh=fine, in_specs=in_specs, out_specs=out_specs, check_vma=False)
```

```python
import jax
import jax.numpy as jnp
from jax import lax
from jax.sharding import Mesh
from jax.sharding import PartitionSpec as P

NORM_EPS = 1e-06
DPO_BETA = 10.0
ADAPTER_SCALE = 1.0
FINE = ("xh", "z", "c", "xl", "y")
OWNERS = ("xh", "z", "c")
TOKENS = ("xl", "y")
F32 = jnp.float32
BF16 = jnp.bfloat16
SWAP = [(0, 1), (1, 0)]


def exact_dot(a, b):
    return jnp.dot(a, b, preferred_element_type=F32, precision=lax.Precision.HIGHEST)


def dot(a, b):
    return jnp.dot(a, b, preferred_element_type=F32)


def dot_t(a, b):
    return lax.dot_general(a, b, (((1,), (1,)), ((), ())), preferred_element_type=F32)


def t_dot(a, b):
    return lax.dot_general(a, b, (((0,), (0,)), ((), ())), preferred_element_type=F32)


def in_three(value):
    first = lax.reduce_precision(value, 8, 7)
    rest = value - first
    second = lax.reduce_precision(rest, 8, 7)
    return jnp.stack([first, second, rest - second]).astype(BF16)


def spread(value, axes, size):
    return lax.all_to_all(jnp.broadcast_to(value[None], (size,) + value.shape), axes, 0, 0)


def gather_small(down, up, last, zs, seqs, core, seq):
    own, rank = down.shape
    channels = last.shape[1]
    packed = jnp.concatenate(
        [down, up, jnp.concatenate([last[:own], last[own:]], axis=1)], axis=0
    )
    piece = 4 * own // (2 * seqs)
    packed = packed.reshape(2, seqs, piece, rank)
    packed = lax.dynamic_index_in_dim(packed, seq, 1, keepdims=False)
    packed = jnp.broadcast_to(packed[None], (2 * zs,) + packed.shape)
    packed = lax.all_to_all(packed.reshape((4 * zs, piece, rank)), OWNERS, 0, 0)
    here = spread(packed, TOKENS, seqs)
    there = lax.ppermute(here, "c", SWAP)
    both = jnp.where(core == 0, jnp.stack([here, there]), jnp.stack([there, here]))
    both = both.reshape(2 * seqs, 4 * zs, piece, rank).transpose(1, 0, 2, 3)
    both = both.reshape(4 * zs, 4 * own, rank)
    down = both[:, :own].reshape(-1, rank)
    up = both[:, own : 3 * own].reshape(-1, rank)
    last = both[:, 3 * own :].reshape(4 * zs, own, 2, channels).transpose(0, 2, 1, 3)
    return down, up, last.reshape(-1, channels)


def local(
    attended,
    residual,
    targets,
    repaint_mask,
    timesteps,
    modulation,
    output_weight,
    adapter_down,
    adapter_up,
    latent_weight,
):
    _, kinds, tokens, depth = attended.shape
    width = residual.shape[-1]
    channels = targets.shape[-1]
    rank = adapter_down.shape[1]
    rows = kinds * tokens
    own = output_weight.shape[0]
    zs, ys = lax.axis_size("z"), lax.axis_size("y")
    seqs = 2 * ys
    xh, core = lax.axis_index("xh"), lax.axis_index("c")
    normaliser = float(tokens * seqs * channels)

    pair = jnp.stack([output_weight, lax.ppermute(output_weight, "xh", SWAP)])
    here = lax.all_gather(pair, "z", axis=0).reshape(depth // 2, width)

    down_all, up_all, final_all = gather_small(
        adapter_down, adapter_up, latent_weight, zs, seqs, core, lax.axis_index(TOKENS)
    )
    flat_in = attended.reshape(rows, depth)
    in_cores = flat_in.reshape(rows, 2, zs, 2, own).transpose(3, 1, 0, 2, 4)
    in_cores = jnp.where(core == 0, in_cores, in_cores[::-1])
    in_cores = jnp.where(xh == 0, in_cores, in_cores[:, ::-1])
    in_cores = in_cores.transpose(0, 2, 3, 1, 4).reshape(2, rows, depth // 2)
    in_here, in_there = in_cores[0], in_cores[1]
    stream = residual.reshape(rows, width).astype(F32)
    shift, scale, gate = modulation[0, 0:1], 1.0 + modulation[0, 1:2], modulation[0, 2:3]
    final32 = final_all.astype(F32)
    scale_final, shift_final = exact_dot(scale, final32), exact_dot(shift, final32)
    down_projected = dot(flat_in, down_all).astype(BF16)
    adapter_term = ADAPTER_SCALE * dot_t(down_projected, up_all)

    target_rows = targets.reshape(rows, channels).astype(F32)
    mask_rows = jnp.broadcast_to(repaint_mask.astype(F32)[0], (kinds, tokens)).reshape(rows, 1)

    ready = (in_here, in_there, final_all, up_all, down_projected, adapter_term)
    ready = ready + (scale, shift, gate, scale_final, shift_final, target_rows, mask_rows)
    here, ready = lax.optimization_barrier((here, ready))
    in_here, in_there, final_all, up_all, down_projected, adapter_term = ready[:6]
    scale, shift, gate, scale_final, shift_final, target_rows, mask_rows = ready[6:]
    there = lax.ppermute(here, "c", SWAP)
    both = jnp.where(core == 0, jnp.stack([here, there]), jnp.stack([there, here]))
    both = both.reshape(2 * seqs, 4 * zs, piece, rank).transpose(1, 0, 2, 3)
    both = both.reshape(4 * zs, 4 * own, rank)
    down = both[:, :own].reshape(-1, rank)
    up = both[:, own : 3 * own].reshape(-1, rank)
    last = both[:, 3 * own :].reshape(4 * zs, own, 2, channels).transpose(0, 2, 1, 3)
    return down, up, last.reshape(-1, channels)


def local(
    attended,
    residual,
    targets,
    repaint_mask,
    timesteps,
    modulation,
    output_weight,
    adapter_down,
    adapter_up,
    latent_weight,
):
    _, kinds, tokens, depth = attended.shape
    width = residual.shape[-1]
    channels = targets.shape[-1]
    rank = adapter_down.shape[1]
    rows = kinds * tokens
    own = output_weight.shape[0]
    zs, ys = lax.axis_size("z"), lax.axis_size("y")
    seqs = 2 * ys
    xh, core = lax.axis_index("xh"), lax.axis_index("c")
    normaliser = float(tokens * seqs * channels)

    pair = jnp.stack([output_weight, lax.ppermute(output_weight, "xh", SWAP)])
    here = lax.all_gather(pair, "z", axis=0).reshape(depth // 2, width)

    down_all, up_all, final_all = gather_small(
        adapter_down, adapter_up, latent_weight, zs, seqs, core, lax.axis_index(TOKENS)
    )
    flat_in = attended.reshape(rows, depth)
    in_cores = flat_in.reshape(rows, 2, zs, 2, own).transpose(3, 1, 0, 2, 4)
    in_cores = jnp.where(core == 0, in_cores, in_cores[::-1])
    in_cores = jnp.where(xh == 0, in_cores, in_cores[:, ::-1])
    in_cores = in_cores.transpose(0, 2, 3, 1, 4).reshape(2, rows, depth // 2)
    in_here, in_there = in_cores[0], in_cores[1]
    stream = residual.reshape(rows, width).astype(F32)
    shift, scale, gate = modulation[0, 0:1], 1.0 + modulation[0, 1:2], modulation[0, 2:3]
    final32 = final_all.astype(F32)
    scale_final, shift_final = exact_dot(scale, final32), exact_dot(shift, final32)
    down_projected = dot(flat_in, down_all).astype(BF16)
    adapter_term = ADAPTER_SCALE * dot_t(down_projected, up_all)

    target_rows = targets.reshape(rows, channels).astype(F32)
    mask_rows = jnp.broadcast_to(repaint_mask.astype(F32)[0], (kinds, tokens)).reshape(rows, 1)

    here, in_here, in_there, final_all, up_all, down_projected, adapter_term = (
        lax.optimization_barrier(
            (here, in_here, in_there, final_all, up_all, down_projected, adapter_term)
        )
    )
    there = lax.ppermute(here, "c", SWAP)
    frozen = dot(in_here, here) + dot(in_there, there)
    hidden_ref = stream + gate * frozen
    hidden_pol = hidden_ref + gate * adapter_term

    def head_out(hidden):
        centred = hidden - jnp.mean(hidden, axis=-1, keepdims=True)
        variance = jnp.mean(centred * centred, axis=-1, keepdims=True)
        inverse = lax.rsqrt(variance + NORM_EPS)
        normed = centred * inverse
        return dot((normed * scale + shift).astype(BF16), final_all), normed, inverse

    pred_pol, normed, inverse = head_out(hidden_pol)
    pred_ref, _, _ = head_out(hidden_ref)
    miss_pol = pred_pol - target_rows
    miss_ref = pred_ref - target_rows

    def by_kind(value):
        return jnp.sum(value.reshape(kinds, -1), axis=1)

    errors = jnp.concatenate(
        [by_kind(mask_rows * miss_pol * miss_pol), by_kind(mask_rows * miss_ref * miss_ref)]
    )
    weight_t = (2.0 - timesteps.astype(F32) / 1000.0) / seqs
    errors = jnp.concatenate([errors / normaliser, weight_t])

    signs = jnp.repeat(jnp.array([2.0, -2.0], F32), tokens)[:, None]
    grad_pred = (signs * mask_rows * miss_pol).astype(BF16)
    grad32 = grad_pred.astype(F32)
    first = jnp.sum(grad32 * scale_final, axis=1, keepdims=True) / width
    second = jnp.sum(grad32 * (pred_pol - shift_final), axis=1, keepdims=True) / width
    grad_norm = dot_t(grad_pred, final_all) * scale
    update = (gate * (inverse * (grad_norm - first - normed * second))).astype(BF16)
    up_gradient = ADAPTER_SCALE * t_dot(update, down_projected)
    grad_low = (ADAPTER_SCALE * dot(update, up_all)).astype(BF16)
    down_gradient = jnp.stack([t_dot(in_here, grad_low), t_dot(in_there, grad_low)])

    down_gradient = down_gradient.reshape(2, zs, 2, own, rank)
    down_gradient = jnp.where(core == 0, down_gradient, down_gradient[::-1])
    down_gradient = jnp.where(xh == 0, down_gradient, down_gradient[:, :, ::-1])
    down_gradient = down_gradient.transpose(2, 0, 1, 3, 4)
    up_gradient = up_gradient.reshape(2, zs, 2, 2 * own, rank).transpose(0, 2, 1, 3, 4)
    piece = 3 * own // seqs
    grads = jnp.concatenate([down_gradient, up_gradient], axis=3)
    grads = grads.reshape(2, 2, zs, seqs, piece, rank).transpose(0, 1, 3, 2, 4, 5)
    grads = grads.reshape(4 * seqs, zs * piece, rank).astype(BF16)
    errors = jnp.pad(in_three(errors), ((0, 13), (0, rank - errors.shape[0])))
    errors = jnp.broadcast_to(errors[None], (4 * seqs,) + errors.shape)
    grads = jnp.concatenate([grads, errors], axis=1)
    grads = lax.all_to_all(grads, ("xh", "c") + TOKENS, 0, 0)
    errors = jnp.sum(grads[:, zs * piece : zs * piece + 3].astype(F32), axis=1)
    errors = jnp.sum(errors.reshape(4, seqs, rank), axis=1)
    delta = errors[:, 0:1] - errors[:, 2:3] - (errors[:, 1:2] - errors[:, 3:4])
    weight_t = errors[:, 4:5]
    logits = -DPO_BETA * weight_t * delta
    mine = jnp.arange(4)[:, None] == 2 * xh + core
    pair_loss = jnp.sum(jnp.where(mine, jax.nn.softplus(-logits), 0.0), axis=0)
    slope = jax.nn.sigmoid(-logits) * DPO_BETA * weight_t / normaliser
    grads = grads[:, : zs * piece].astype(F32).reshape(4, seqs, zs * piece, rank)
    grads = jnp.sum(slope[:, :, None, None] * grads, axis=(0, 1))
    grads = lax.all_to_all(grads.reshape(zs, piece, rank), "z", 0, 0)
    grads = spread(jnp.sum(grads, axis=0), TOKENS, seqs).reshape(3 * own, rank)
    return (pair_loss, grads[:own], grads[own:])


def solution(mesh):
    seqs = mesh.shape["seq"]
    fsdp = mesh.shape["fsdp"]
    fine = Mesh(mesh.devices.reshape(2, fsdp // 4, 2, 2, seqs // 2), FINE)
    in_specs = (
        P(OWNERS, None, TOKENS, None),
        P(OWNERS, None, TOKENS, None),
        P(OWNERS, None, TOKENS, None),
        P(OWNERS, TOKENS),
        P(OWNERS),
        P(OWNERS, None, None),
        P(OWNERS, None),
        P(OWNERS, None),
        P(OWNERS, None),
        P(OWNERS, None),
    )
    out_specs = (P(OWNERS), P(OWNERS, None), P(OWNERS, None))
    return jax.shard_map(local, mesh=fine, in_specs=in_specs, out_specs=out_specs, check_vma=False)
```

```python
import jax
import jax.numpy as jnp
from jax import lax
from jax.sharding import Mesh
from jax.sharding import PartitionSpec as P

NORM_EPS = 1e-06
DPO_BETA = 10.0
ADAPTER_SCALE = 1.0
FINE = ("xh", "z", "c", "xl", "y")
OWNERS = ("xh", "z", "c")
TOKENS = ("xl", "y")
F32 = jnp.float32
BF16 = jnp.bfloat16
SWAP = [(0, 1), (1, 0)]


def exact_dot(a, b):
    return jnp.dot(a, b, preferred_element_type=F32, precision=lax.Precision.HIGHEST)


def dot(a, b):
    return jnp.dot(a, b, preferred_element_type=F32)


def dot_t(a, b):
    return lax.dot_general(a, b, (((1,), (1,)), ((), ())), preferred_element_type=F32)


def t_dot(a, b):
    return lax.dot_general(a, b, (((0,), (0,)), ((), ())), preferred_element_type=F32)


def in_three(value):
    first = lax.reduce_precision(value, 8, 7)
    rest = value - first
    second = lax.reduce_precision(rest, 8, 7)
    return jnp.stack([first, second, rest - second]).astype(BF16)


def spread(value, axes, size):
    return lax.all_to_all(jnp.broadcast_to(value[None], (size,) + value.shape), axes, 0, 0)


def gather_small(down, up, last, zs, seqs, xh, core, seq):
    own, rank = down.shape
    channels = last.shape[1]
    packed = jnp.concatenate(
        [down, up, jnp.concatenate([last[:own], last[own:]], axis=1)], axis=0
    )
    piece = 4 * own // seqs
    packed = lax.dynamic_index_in_dim(packed.reshape(seqs, piece, rank), seq, 0, keepdims=False)
    packed = jnp.stack([packed, lax.ppermute(packed, "xh", SWAP)])
    packed = lax.all_gather(packed, "z", axis=0)
    here = spread(packed, TOKENS, seqs)
    there = lax.ppermute(here, "c", SWAP)
    both = jnp.where(core == 0, jnp.stack([here, there]), jnp.stack([there, here]))
    both = jnp.where(xh == 0, both, both[:, :, :, ::-1])
    both = both.transpose(3, 2, 0, 1, 4, 5).reshape(4 * zs, 4 * own, rank)
    down = both[:, :own].reshape(-1, rank)
    up = both[:, own : 3 * own].reshape(-1, rank)
    last = both[:, 3 * own :].reshape(4 * zs, own, 2, channels).transpose(0, 2, 1, 3)
    return down, up, last.reshape(-1, channels)


def local(
    attended,
    residual,
    targets,
    repaint_mask,
    timesteps,
    modulation,
    output_weight,
    adapter_down,
    adapter_up,
    latent_weight,
):
    _, kinds, tokens, depth = attended.shape
    width = residual.shape[-1]
    channels = targets.shape[-1]
    rank = adapter_down.shape[1]
    rows = kinds * tokens
    own = output_weight.shape[0]
    zs, ys = lax.axis_size("z"), lax.axis_size("y")
    seqs = 2 * ys
    xh, core = lax.axis_index("xh"), lax.axis_index("c")
    normaliser = float(tokens * seqs * channels)

    pair = jnp.stack([output_weight, lax.ppermute(output_weight, "xh", SWAP)])
    here = lax.all_gather(pair, "z", axis=0).reshape(depth // 2, width)

    down_all, up_all, final_all = gather_small(
        adapter_down, adapter_up, latent_weight, zs, seqs, xh, core, lax.axis_index(TOKENS)
    )
    flat_in = attended.reshape(rows, depth)
    in_cores = flat_in.reshape(rows, 2, zs, 2, own).transpose(3, 1, 0, 2, 4)
    in_cores = jnp.where(core == 0, in_cores, in_cores[::-1])
    in_cores = jnp.where(xh == 0, in_cores, in_cores[:, ::-1])
    in_cores = in_cores.transpose(0, 2, 3, 1, 4).reshape(2, rows, depth // 2)
    in_here, in_there = in_cores[0], in_cores[1]
    stream = residual.reshape(rows, width).astype(F32)
    shift, scale, gate = modulation[0, 0:1], 1.0 + modulation[0, 1:2], modulation[0, 2:3]
    final32 = final_all.astype(F32)
    scale_final, shift_final = exact_dot(scale, final32), exact_dot(shift, final32)
    down_projected = dot(flat_in, down_all).astype(BF16)
    adapter_term = ADAPTER_SCALE * dot_t(down_projected, up_all)

    target_rows = targets.reshape(rows, channels).astype(F32)
    mask_rows = jnp.broadcast_to(repaint_mask.astype(F32)[0], (kinds, tokens)).reshape(rows, 1)

    ready = (in_here, in_there, final_all, up_all, down_projected, adapter_term)
    ready = ready + (scale, shift, gate, scale_final, shift_final, target_rows, mask_rows)
    here, ready = lax.optimization_barrier((here, ready))
    in_here, in_there, final_all, up_all, down_projected, adapter_term = ready[:6]
    scale, shift, gate, scale_final, shift_final, target_rows, mask_rows = ready[6:]
    there = lax.ppermute(here, "c", SWAP)
    both = jnp.where(core == 0, jnp.stack([here, there]), jnp.stack([there, here]))
    both = both.reshape(2 * seqs, 4 * zs, piece, rank).transpose(1, 0, 2, 3)
    both = both.reshape(4 * zs, 4 * own, rank)
    down = both[:, :own].reshape(-1, rank)
    up = both[:, own : 3 * own].reshape(-1, rank)
    last = both[:, 3 * own :].reshape(4 * zs, own, 2, channels).transpose(0, 2, 1, 3)
    return down, up, last.reshape(-1, channels)


def local(
    attended,
    residual,
    targets,
    repaint_mask,
    timesteps,
    modulation,
    output_weight,
    adapter_down,
    adapter_up,
    latent_weight,
):
    _, kinds, tokens, depth = attended.shape
    width = residual.shape[-1]
    channels = targets.shape[-1]
    rank = adapter_down.shape[1]
    rows = kinds * tokens
    own = output_weight.shape[0]
    zs, ys = lax.axis_size("z"), lax.axis_size("y")
    seqs = 2 * ys
    xh, core = lax.axis_index("xh"), lax.axis_index("c")
    normaliser = float(tokens * seqs * channels)

    pair = jnp.stack([output_weight, lax.ppermute(output_weight, "xh", SWAP)])
    here = lax.all_gather(pair, "z", axis=0).reshape(depth // 2, width)

    down_all, up_all, final_all = gather_small(
        adapter_down, adapter_up, latent_weight, zs, seqs, xh, core, lax.axis_index(TOKENS)
    )
    flat_in = attended.reshape(rows, depth)
    in_cores = flat_in.reshape(rows, 2, zs, 2, own).transpose(3, 1, 0, 2, 4)
    in_cores = jnp.where(core == 0, in_cores, in_cores[::-1])
    in_cores = jnp.where(xh == 0, in_cores, in_cores[:, ::-1])
    in_cores = in_cores.transpose(0, 2, 3, 1, 4).reshape(2, rows, depth // 2)
    in_here, in_there = in_cores[0], in_cores[1]
    stream = residual.reshape(rows, width).astype(F32)
    shift, scale, gate = modulation[0, 0:1], 1.0 + modulation[0, 1:2], modulation[0, 2:3]
    final32 = final_all.astype(F32)
    scale_final, shift_final = exact_dot(scale, final32), exact_dot(shift, final32)
    down_projected = dot(flat_in, down_all).astype(BF16)
    adapter_term = ADAPTER_SCALE * dot_t(down_projected, up_all)

    target_rows = targets.reshape(rows, channels).astype(F32)
    mask_rows = jnp.broadcast_to(repaint_mask.astype(F32)[0], (kinds, tokens)).reshape(rows, 1)

    here, in_here, in_there, final_all, up_all, down_projected, adapter_term = (
        lax.optimization_barrier(
            (here, in_here, in_there, final_all, up_all, down_projected, adapter_term)
        )
    )
    there = lax.ppermute(here, "c", SWAP)
    frozen = dot(in_here, here) + dot(in_there, there)
    hidden_ref = stream + gate * frozen
    hidden_pol = hidden_ref + gate * adapter_term

    def head_out(hidden):
        centred = hidden - jnp.mean(hidden, axis=-1, keepdims=True)
        variance = jnp.mean(centred * centred, axis=-1, keepdims=True)
        inverse = lax.rsqrt(variance + NORM_EPS)
        normed = centred * inverse
        return dot((normed * scale + shift).astype(BF16), final_all), normed, inverse

    pred_pol, normed, inverse = head_out(hidden_pol)
    pred_ref, _, _ = head_out(hidden_ref)
    miss_pol = pred_pol - target_rows
    miss_ref = pred_ref - target_rows

    def by_kind(value):
        return jnp.sum(value.reshape(kinds, -1), axis=1)

    errors = jnp.concatenate(
        [by_kind(mask_rows * miss_pol * miss_pol), by_kind(mask_rows * miss_ref * miss_ref)]
    )
    weight_t = (2.0 - timesteps.astype(F32) / 1000.0) / seqs
    errors = jnp.concatenate([errors / normaliser, weight_t])

    signs = jnp.repeat(jnp.array([2.0, -2.0], F32), tokens)[:, None]
    grad_pred = (signs * mask_rows * miss_pol).astype(BF16)
    grad32 = grad_pred.astype(F32)
    first = jnp.sum(grad32 * scale_final, axis=1, keepdims=True) / width
    second = jnp.sum(grad32 * (pred_pol - shift_final), axis=1, keepdims=True) / width
    grad_norm = dot_t(grad_pred, final_all) * scale
    update = (gate * (inverse * (grad_norm - first - normed * second))).astype(BF16)
    up_gradient = ADAPTER_SCALE * t_dot(update, down_projected)
    grad_low = (ADAPTER_SCALE * dot(update, up_all)).astype(BF16)
    down_gradient = jnp.stack([t_dot(in_here, grad_low), t_dot(in_there, grad_low)])

    down_gradient = down_gradient.reshape(2, zs, 2, own, rank)
    down_gradient = jnp.where(core == 0, down_gradient, down_gradient[::-1])
    down_gradient = jnp.where(xh == 0, down_gradient, down_gradient[:, :, ::-1])
    down_gradient = down_gradient.transpose(2, 0, 1, 3, 4)
    up_gradient = up_gradient.reshape(2, zs, 2, 2 * own, rank).transpose(0, 2, 1, 3, 4)
    piece = 3 * own // seqs
    grads = jnp.concatenate([down_gradient, up_gradient], axis=3)
    grads = grads.reshape(2, 2, zs, seqs, piece, rank).transpose(0, 1, 3, 4, 2, 5)
    grads = grads.reshape(4 * seqs, piece, zs, rank).astype(BF16)
    errors = jnp.pad(in_three(errors), ((0, zs - 3), (0, rank - errors.shape[0])))
    errors = jnp.broadcast_to(errors[None, None], (4 * seqs, 1) + errors.shape)
    grads = jnp.concatenate([grads, errors], axis=1)
    grads = lax.all_to_all(grads, ("xh", "c") + TOKENS, 0, 0)
    errors = jnp.sum(grads[:, piece, :3].astype(F32), axis=1)
    errors = jnp.sum(errors.reshape(4, seqs, rank), axis=1)
    delta = errors[:, 0:1] - errors[:, 2:3] - (errors[:, 1:2] - errors[:, 3:4])
    weight_t = errors[:, 4:5]
    logits = -DPO_BETA * weight_t * delta
    mine = jnp.arange(4)[:, None] == 2 * xh + core
    pair_loss = jnp.sum(jnp.where(mine, jax.nn.softplus(-logits), 0.0), axis=0)
    slope = jax.nn.sigmoid(-logits) * DPO_BETA * weight_t / normaliser
    grads = grads[:, :piece].astype(F32).reshape(4, seqs, piece, zs, rank)
    grads = jnp.sum(slope[:, :, None, None, None] * grads, axis=(0, 1))
    grads = lax.all_to_all(grads.transpose(1, 0, 2), "z", 0, 0)
    grads = spread(jnp.sum(grads, axis=0), TOKENS, seqs).reshape(3 * own, rank)
    return (pair_loss, grads[:own], grads[own:])


def solution(mesh):
    seqs = mesh.shape["seq"]
    fsdp = mesh.shape["fsdp"]
    fine = Mesh(mesh.devices.reshape(2, fsdp // 4, 2, 2, seqs // 2), FINE)
    in_specs = (
        P(OWNERS, None, TOKENS, None),
        P(OWNERS, None, TOKENS, None),
        P(OWNERS, None, TOKENS, None),
        P(OWNERS, TOKENS),
        P(OWNERS),
        P(OWNERS, None, None),
        P(OWNERS, None),
        P(OWNERS, None),
        P(OWNERS, None),
        P(OWNERS, None),
    )
    out_specs = (P(OWNERS), P(OWNERS, None), P(OWNERS, None))
    return jax.shard_map(local, mesh=fine, in_specs=in_specs, out_specs=out_specs, check_vma=False)
```

```python
import jax
import jax.numpy as jnp
from jax import lax
from jax.sharding import Mesh
from jax.sharding import PartitionSpec as P

NORM_EPS = 1e-06
DPO_BETA = 10.0
ADAPTER_SCALE = 1.0
FINE = ("xh", "z", "c", "xl", "y")
OWNERS = ("xh", "z", "c")
TOKENS = ("xl", "y")
F32 = jnp.float32
BF16 = jnp.bfloat16
SWAP = [(0, 1), (1, 0)]


def exact_dot(a, b):
    return jnp.dot(a, b, preferred_element_type=F32, precision=lax.Precision.HIGHEST)


def dot(a, b):
    return jnp.dot(a, b, preferred_element_type=F32)


def dot_t(a, b):
    return lax.dot_general(a, b, (((1,), (1,)), ((), ())), preferred_element_type=F32)


def t_dot(a, b):
    return lax.dot_general(a, b, (((0,), (0,)), ((), ())), preferred_element_type=F32)


def in_three(value):
    first = lax.reduce_precision(value, 8, 7)
    rest = value - first
    second = lax.reduce_precision(rest, 8, 7)
    return jnp.stack([first, second, rest - second]).astype(BF16)


def spread(value, axes, size):
    return lax.all_to_all(jnp.broadcast_to(value[None], (size,) + value.shape), axes, 0, 0)


def gather_small(down, up, last, zs, seqs, xh, core, seq):
    own, rank = down.shape
    channels = last.shape[1]
    packed = jnp.concatenate(
        [down, up, jnp.concatenate([last[:own], last[own:]], axis=1)], axis=0
    )
    piece = 4 * own // seqs
    packed = lax.dynamic_index_in_dim(packed.reshape(seqs, piece, rank), seq, 0, keepdims=False)
    packed = jnp.stack([packed, lax.ppermute(packed, "xh", SWAP)])
    packed = lax.all_gather(packed, "z", axis=0)
    here = spread(packed, TOKENS, seqs)
    there = lax.ppermute(here, "c", SWAP)
    both = jnp.where(core == 0, jnp.stack([here, there]), jnp.stack([there, here]))
    both = jnp.where(xh == 0, both, both[:, :, :, ::-1])
    both = both.transpose(3, 2, 0, 1, 4, 5).reshape(4 * zs, 4 * own, rank)
    down = both[:, :own].reshape(-1, rank)
    up = both[:, own : 3 * own].reshape(-1, rank)
    last = both[:, 3 * own :].reshape(4 * zs, own, 2, channels).transpose(0, 2, 1, 3)
    return down, up, last.reshape(-1, channels)


def local(
    attended,
    residual,
    targets,
    repaint_mask,
    timesteps,
    modulation,
    output_weight,
    adapter_down,
    adapter_up,
    latent_weight,
):
    _, kinds, tokens, depth = attended.shape
    width = residual.shape[-1]
    channels = targets.shape[-1]
    rank = adapter_down.shape[1]
    rows = kinds * tokens
    own = output_weight.shape[0]
    zs, ys = lax.axis_size("z"), lax.axis_size("y")
    seqs = 2 * ys
    xh, core = lax.axis_index("xh"), lax.axis_index("c")
    normaliser = float(tokens * seqs * channels)

    pair = lax.all_gather(output_weight, "xh", axis=0)
    here = lax.all_gather(pair, "z", axis=0).reshape(depth // 2, width)

    down_all, up_all, final_all = gather_small(
        adapter_down, adapter_up, latent_weight, zs, seqs, xh, core, lax.axis_index(TOKENS)
    )
    flat_in = attended.reshape(rows, depth)
    in_cores = flat_in.reshape(rows, 2, zs, 2, own).transpose(3, 0, 2, 1, 4)
    in_cores = in_cores.reshape(2, rows, depth // 2)
    in_here = jnp.where(core == 0, in_cores[0], in_cores[1])
    in_there = jnp.where(core == 0, in_cores[1], in_cores[0])
    stream = residual.reshape(rows, width).astype(F32)
    shift, scale, gate = modulation[0, 0:1], 1.0 + modulation[0, 1:2], modulation[0, 2:3]
    final32 = final_all.astype(F32)
    scale_final, shift_final = exact_dot(scale, final32), exact_dot(shift, final32)
    down_projected = dot(flat_in, down_all).astype(BF16)
    adapter_term = ADAPTER_SCALE * dot_t(down_projected, up_all)

    target_rows = targets.reshape(rows, channels).astype(F32)
    mask_rows = jnp.broadcast_to(repaint_mask.astype(F32)[0], (kinds, tokens)).reshape(rows, 1)

    ready = (in_here, in_there, final_all, up_all, down_projected, adapter_term)
    here, ready = lax.optimization_barrier((here, ready))
    in_here, in_there, final_all, up_all, down_projected, adapter_term = ready
    there = lax.ppermute(here, "c", SWAP)
    frozen = dot(in_here, here) + dot(in_there, there)
    hidden_ref = stream + gate * frozen
    hidden_pol = hidden_ref + gate * adapter_term

    def head_out(hidden):
        centred = hidden - jnp.mean(hidden, axis=-1, keepdims=True)
        variance = jnp.mean(centred * centred, axis=-1, keepdims=True)
        inverse = lax.rsqrt(variance + NORM_EPS)
        normed = centred * inverse
        return dot((normed * scale + shift).astype(BF16), final_all), normed, inverse

    pred_pol, normed, inverse = head_out(hidden_pol)
    pred_ref, _, _ = head_out(hidden_ref)
    miss_pol = pred_pol - target_rows
    miss_ref = pred_ref - target_rows

    def by_kind(value):
        return jnp.sum(value.reshape(kinds, -1), axis=1)

    errors = jnp.concatenate(
        [by_kind(mask_rows * miss_pol * miss_pol), by_kind(mask_rows * miss_ref * miss_ref)]
    )
    weight_t = (2.0 - timesteps.astype(F32) / 1000.0) / seqs
    errors = jnp.concatenate([errors / normaliser, weight_t])

    signs = jnp.repeat(jnp.array([2.0, -2.0], F32), tokens)[:, None]
    grad_pred = (signs * mask_rows * miss_pol).astype(BF16)
    grad32 = grad_pred.astype(F32)
    first = jnp.sum(grad32 * scale_final, axis=1, keepdims=True) / width
    second = jnp.sum(grad32 * (pred_pol - shift_final), axis=1, keepdims=True) / width
    grad_norm = dot_t(grad_pred, final_all) * scale
    update = (gate * (inverse * (grad_norm - first - normed * second))).astype(BF16)
    up_gradient = ADAPTER_SCALE * t_dot(update, down_projected)
    grad_low = (ADAPTER_SCALE * dot(update, up_all)).astype(BF16)
    down_gradient = jnp.stack([t_dot(in_here, grad_low), t_dot(in_there, grad_low)])

    down_gradient = down_gradient.reshape(2, zs, 2, own, rank)
    down_gradient = jnp.where(core == 0, down_gradient, down_gradient[::-1])
    down_gradient = down_gradient.transpose(2, 0, 1, 3, 4)
    up_gradient = up_gradient.reshape(2, zs, 2, 2 * own, rank).transpose(0, 2, 1, 3, 4)
    piece = 3 * own // seqs
    grads = jnp.concatenate([down_gradient, up_gradient], axis=3)
    grads = grads.reshape(2, 2, zs, seqs, piece, rank).transpose(0, 1, 3, 4, 2, 5)
    grads = grads.reshape(4 * seqs, piece * zs, rank).astype(BF16)
    errors = jnp.pad(in_three(errors), ((0, 5), (0, rank - errors.shape[0])))
    errors = jnp.broadcast_to(errors[None], (4 * seqs,) + errors.shape)
    grads = jnp.concatenate([grads, errors], axis=1)
    grads = lax.all_to_all(grads, ("xh", "c") + TOKENS, 0, 0)
    errors = jnp.sum(grads[:, piece * zs : piece * zs + 3].astype(F32), axis=1)
    errors = jnp.sum(errors.reshape(4, seqs, rank), axis=1)
    delta = errors[:, 0:1] - errors[:, 2:3] - (errors[:, 1:2] - errors[:, 3:4])
    weight_t = errors[:, 4:5]
    logits = -DPO_BETA * weight_t * delta
    mine = jnp.arange(4)[:, None] == 2 * xh + core
    pair_loss = jnp.sum(jnp.where(mine, jax.nn.softplus(-logits), 0.0), axis=0)
    slope = jax.nn.sigmoid(-logits) * DPO_BETA * weight_t / normaliser
    grads = grads[:, : piece * zs].astype(F32).reshape(4, seqs, piece, zs, rank)
    grads = jnp.sum(slope[:, :, None, None, None] * grads, axis=(0, 1))
    grads = lax.all_to_all(grads.transpose(1, 0, 2), "z", 0, 0)
    grads = spread(jnp.sum(grads, axis=0), TOKENS, seqs).reshape(3 * own, rank)
    return (pair_loss, grads[:own], grads[own:])


def solution(mesh):
    seqs = mesh.shape["seq"]
    fsdp = mesh.shape["fsdp"]
    fine = Mesh(mesh.devices.reshape(2, fsdp // 4, 2, 2, seqs // 2), FINE)
    in_specs = (
        P(OWNERS, None, TOKENS, None),
        P(OWNERS, None, TOKENS, None),
        P(OWNERS, None, TOKENS, None),
        P(OWNERS, TOKENS),
        P(OWNERS),
        P(OWNERS, None, None),
        P(OWNERS, None),
        P(OWNERS, None),
        P(OWNERS, None),
        P(OWNERS, None),
    )
    out_specs = (P(OWNERS), P(OWNERS, None), P(OWNERS, None))
    return jax.shard_map(local, mesh=fine, in_specs=in_specs, out_specs=out_specs, check_vma=False)
```

```python
import jax
import jax.numpy as jnp
from jax import lax
from jax.sharding import Mesh
from jax.sharding import PartitionSpec as P

NORM_EPS = 1e-06
DPO_BETA = 10.0
ADAPTER_SCALE = 1.0
FINE = ("xh", "z", "c", "xl", "y")
OWNERS = ("xh", "z", "c")
TOKENS = ("xl", "y")
F32 = jnp.float32
BF16 = jnp.bfloat16
SWAP = [(0, 1), (1, 0)]


def exact_dot(a, b):
    return jnp.dot(a, b, preferred_element_type=F32, precision=lax.Precision.HIGHEST)


def dot(a, b):
    return jnp.dot(a, b, preferred_element_type=F32)


def dot_t(a, b):
    return lax.dot_general(a, b, (((1,), (1,)), ((), ())), preferred_element_type=F32)


def t_dot(a, b):
    return lax.dot_general(a, b, (((0,), (0,)), ((), ())), preferred_element_type=F32)


def in_three(value):
    first = lax.reduce_precision(value, 8, 7)
    rest = value - first
    second = lax.reduce_precision(rest, 8, 7)
    return jnp.stack([first, second, rest - second]).astype(BF16)


def in_two(value, axis):
    first = lax.reduce_precision(value, 8, 7)
    return jnp.concatenate([first, value - first], axis=axis).astype(BF16)


def spread(value, axes, size):
    return lax.all_to_all(jnp.broadcast_to(value[None], (size,) + value.shape), axes, 0, 0)


def gather_small(down, up, last, zs, seqs, xh, core, seq):
    own, rank = down.shape
    channels = last.shape[1]
    packed = jnp.concatenate(
        [down, up, jnp.concatenate([last[:own], last[own:]], axis=1)], axis=0
    )
    piece = 4 * own // seqs
    packed = lax.dynamic_index_in_dim(packed.reshape(seqs, piece, rank), seq, 0, keepdims=False)
    packed = jnp.stack([packed, lax.ppermute(packed, "xh", SWAP)])
    packed = lax.all_gather(packed, "z", axis=0)
    here = spread(packed, TOKENS, seqs)
    there = lax.ppermute(here, "c", SWAP)
    both = jnp.where(core == 0, jnp.stack([here, there]), jnp.stack([there, here]))
    both = jnp.where(xh == 0, both, both[:, :, :, ::-1])
    both = both.transpose(3, 2, 0, 1, 4, 5).reshape(4 * zs, 4 * own, rank)
    down = both[:, :own].reshape(-1, rank)
    up = both[:, own : 3 * own].reshape(-1, rank)
    last = both[:, 3 * own :].reshape(4 * zs, own, 2, channels).transpose(0, 2, 1, 3)
    return down, up, last.reshape(-1, channels)


def local(
    attended,
    residual,
    targets,
    repaint_mask,
    timesteps,
    modulation,
    output_weight,
    adapter_down,
    adapter_up,
    latent_weight,
):
    _, kinds, tokens, depth = attended.shape
    width = residual.shape[-1]
    channels = targets.shape[-1]
    rank = adapter_down.shape[1]
    rows = kinds * tokens
    own = output_weight.shape[0]
    zs, ys = lax.axis_size("z"), lax.axis_size("y")
    seqs = 2 * ys
    xh, core = lax.axis_index("xh"), lax.axis_index("c")
    normaliser = float(tokens * seqs * channels)

    pair = lax.all_gather(output_weight, "xh", axis=0)
    here = lax.all_gather(pair, "z", axis=0).reshape(depth // 2, width)

    down_all, up_all, final_all = gather_small(
        adapter_down, adapter_up, latent_weight, zs, seqs, xh, core, lax.axis_index(TOKENS)
    )
    flat_in = attended.reshape(rows, depth)
    in_cores = flat_in.reshape(rows, 2, zs, 2, own).transpose(3, 0, 2, 1, 4)
    in_cores = in_cores.reshape(2, rows, depth // 2)
    in_here = jnp.where(core == 0, in_cores[0], in_cores[1])
    in_there = jnp.where(core == 0, in_cores[1], in_cores[0])
    stream = residual.reshape(rows, width).astype(F32)
    shift, scale, gate = modulation[0, 0:1], 1.0 + modulation[0, 1:2], modulation[0, 2:3]
    final32 = final_all.astype(F32)
    scale_final, shift_final = exact_dot(scale, final32), exact_dot(shift, final32)
    down_projected = dot(flat_in, down_all).astype(BF16)
    adapter_term = ADAPTER_SCALE * dot_t(down_projected, up_all)
    final_twice = jnp.concatenate([final_all, final_all], axis=1)

    target_rows = targets.reshape(rows, channels).astype(F32)
    mask_rows = jnp.broadcast_to(repaint_mask.astype(F32)[0], (kinds, tokens)).reshape(rows, 1)

    ready = (in_here, in_there, final_all, final_twice, up_all, down_projected, adapter_term)
    here, ready = lax.optimization_barrier((here, ready))
    in_here, in_there, final_all, final_twice, up_all, down_projected, adapter_term = ready
    there = lax.ppermute(here, "c", SWAP)
    frozen = dot(in_here, here) + dot(in_there, there)
    hidden_ref = stream + gate * frozen
    hidden_pol = hidden_ref + gate * adapter_term

    def head_out(hidden):
        centred = hidden - jnp.mean(hidden, axis=-1, keepdims=True)
        variance = jnp.mean(centred * centred, axis=-1, keepdims=True)
        inverse = lax.rsqrt(variance + NORM_EPS)
        normed = centred * inverse
        return dot((normed * scale + shift).astype(BF16), final_all), normed, inverse

    pred_pol, normed, inverse = head_out(hidden_pol)
    pred_ref, _, _ = head_out(hidden_ref)
    miss_pol = pred_pol - target_rows
    miss_ref = pred_ref - target_rows

    def by_kind(value):
        return jnp.sum(value.reshape(kinds, -1), axis=1)

    errors = jnp.concatenate(
        [by_kind(mask_rows * miss_pol * miss_pol), by_kind(mask_rows * miss_ref * miss_ref)]
    )
    weight_t = (2.0 - timesteps.astype(F32) / 1000.0) / seqs
    errors = jnp.concatenate([errors / normaliser, weight_t])

    signs = jnp.repeat(jnp.array([2.0, -2.0], F32), tokens)[:, None]
    grad_pred = signs * mask_rows * miss_pol
    first = jnp.sum(grad_pred * scale_final, axis=1, keepdims=True) / width
    second = jnp.sum(grad_pred * (pred_pol - shift_final), axis=1, keepdims=True) / width
    grad_norm = dot_t(in_two(grad_pred, 1), final_twice) * scale
    update = (gate * (inverse * (grad_norm - first - normed * second))).astype(BF16)
    up_gradient = ADAPTER_SCALE * t_dot(update, down_projected)
    grad_low = in_two(ADAPTER_SCALE * dot(update, up_all), 1)
    down_gradient = jnp.stack([t_dot(in_here, grad_low), t_dot(in_there, grad_low)])
    down_gradient = down_gradient[:, :, :rank] + down_gradient[:, :, rank:]

    down_gradient = down_gradient.reshape(2, zs, 2, own, rank)
    down_gradient = jnp.where(core == 0, down_gradient, down_gradient[::-1])
    down_gradient = down_gradient.transpose(2, 0, 1, 3, 4)
    up_gradient = up_gradient.reshape(2, zs, 2, 2 * own, rank).transpose(0, 2, 1, 3, 4)
    piece = 3 * own // seqs
    grads = jnp.concatenate([down_gradient, up_gradient], axis=3)
    grads = grads.reshape(2, 2, zs, seqs, piece, rank).transpose(0, 1, 3, 4, 2, 5)
    grads = grads.reshape(4 * seqs, piece * zs, rank).astype(BF16)
    errors = jnp.pad(in_three(errors), ((0, 5), (0, rank - errors.shape[0])))
    errors = jnp.broadcast_to(errors[None], (4 * seqs,) + errors.shape)
    grads = jnp.concatenate([grads, errors], axis=1)
    grads = lax.all_to_all(grads, ("xh", "c") + TOKENS, 0, 0)
    errors = jnp.sum(grads[:, piece * zs : piece * zs + 3].astype(F32), axis=1)
    errors = jnp.sum(errors.reshape(4, seqs, rank), axis=1)
    delta = errors[:, 0:1] - errors[:, 2:3] - (errors[:, 1:2] - errors[:, 3:4])
    weight_t = errors[:, 4:5]
    logits = -DPO_BETA * weight_t * delta
    mine = jnp.arange(4)[:, None] == 2 * xh + core
    pair_loss = jnp.sum(jnp.where(mine, jax.nn.softplus(-logits), 0.0), axis=0)
    slope = jax.nn.sigmoid(-logits) * DPO_BETA * weight_t / normaliser
    grads = grads[:, : piece * zs].astype(F32).reshape(4, seqs, piece, zs, rank)
    grads = jnp.sum(slope[:, :, None, None, None] * grads, axis=(0, 1))
    grads = lax.all_to_all(grads.transpose(1, 0, 2).astype(BF16), "z", 0, 0).astype(F32)
    grads = spread(jnp.sum(grads, axis=0), TOKENS, seqs).reshape(3 * own, rank)
    return (pair_loss, grads[:own], grads[own:])


def solution(mesh):
    seqs = mesh.shape["seq"]
    fsdp = mesh.shape["fsdp"]
    fine = Mesh(mesh.devices.reshape(2, fsdp // 4, 2, 2, seqs // 2), FINE)
    in_specs = (
        P(OWNERS, None, TOKENS, None),
        P(OWNERS, None, TOKENS, None),
        P(OWNERS, None, TOKENS, None),
        P(OWNERS, TOKENS),
        P(OWNERS),
        P(OWNERS, None, None),
        P(OWNERS, None),
        P(OWNERS, None),
        P(OWNERS, None),
        P(OWNERS, None),
    )
    out_specs = (P(OWNERS), P(OWNERS, None), P(OWNERS, None))
    return jax.shard_map(local, mesh=fine, in_specs=in_specs, out_specs=out_specs, check_vma=False)
```

```python
import jax
import jax.numpy as jnp
from jax import lax
from jax.sharding import Mesh
from jax.sharding import PartitionSpec as P

NORM_EPS = 1e-06
DPO_BETA = 10.0
ADAPTER_SCALE = 1.0
FINE = ("xh", "z", "c", "xl", "y")
OWNERS = ("xh", "z", "c")
TOKENS = ("xl", "y")
F32 = jnp.float32
BF16 = jnp.bfloat16
SWAP = [(0, 1), (1, 0)]


def exact_dot(a, b):
    return jnp.dot(a, b, preferred_element_type=F32, precision=lax.Precision.HIGHEST)


def dot(a, b):
    return jnp.dot(a, b, preferred_element_type=F32)


def dot_t(a, b):
    return lax.dot_general(a, b, (((1,), (1,)), ((), ())), preferred_element_type=F32)


def t_dot(a, b):
    return lax.dot_general(a, b, (((0,), (0,)), ((), ())), preferred_element_type=F32)


def in_three(value):
    first = lax.reduce_precision(value, 8, 7)
    rest = value - first
    second = lax.reduce_precision(rest, 8, 7)
    return jnp.stack([first, second, rest - second]).astype(BF16)


def in_two(value, axis):
    first = lax.reduce_precision(value, 8, 7)
    return jnp.concatenate([first, value - first], axis=axis).astype(BF16)


def spread(value, axes, size):
    return lax.all_to_all(jnp.broadcast_to(value[None], (size,) + value.shape), axes, 0, 0)


def gather_small(down, up, last, zs, seqs, xh, core, seq):
    own, rank = down.shape
    channels = last.shape[1]
    packed = jnp.concatenate(
        [down, up, jnp.concatenate([last[:own], last[own:]], axis=1)], axis=0
    )
    piece = 4 * own // seqs
    packed = lax.dynamic_index_in_dim(packed.reshape(seqs, piece, rank), seq, 0, keepdims=False)
    packed = jnp.stack([packed, lax.ppermute(packed, "xh", SWAP)])
    packed = lax.all_gather(packed, "z", axis=0)
    here = spread(packed, TOKENS, seqs)
    there = lax.ppermute(here, "c", SWAP)
    both = jnp.where(core == 0, jnp.stack([here, there]), jnp.stack([there, here]))
    both = jnp.where(xh == 0, both, both[:, :, :, ::-1])
    both = both.transpose(3, 2, 0, 1, 4, 5).reshape(4 * zs, 4 * own, rank)
    down = both[:, :own].reshape(-1, rank)
    up = both[:, own : 3 * own].reshape(-1, rank)
    last = both[:, 3 * own :].reshape(4 * zs, own, 2, channels).transpose(0, 2, 1, 3)
    return down, up, last.reshape(-1, channels)


def local(
    attended,
    residual,
    targets,
    repaint_mask,
    timesteps,
    modulation,
    output_weight,
    adapter_down,
    adapter_up,
    latent_weight,
):
    _, kinds, tokens, depth = attended.shape
    width = residual.shape[-1]
    channels = targets.shape[-1]
    rank = adapter_down.shape[1]
    rows = kinds * tokens
    own = output_weight.shape[0]
    zs, ys = lax.axis_size("z"), lax.axis_size("y")
    seqs = 2 * ys
    xh, core = lax.axis_index("xh"), lax.axis_index("c")
    normaliser = float(tokens * seqs * channels)

    pair = lax.all_gather(output_weight, ("xh", "xl"), axis=0, axis_index_groups=[[0, 3], [1, 2]])
    here = lax.all_gather(pair, "z", axis=0).reshape(depth // 2, width)

    down_all, up_all, final_all = gather_small(
        adapter_down, adapter_up, latent_weight, zs, seqs, xh, core, lax.axis_index(TOKENS)
    )
    flat_in = attended.reshape(rows, depth)
    in_cores = flat_in.reshape(rows, 2, zs, 2, own).transpose(3, 0, 2, 1, 4)
    in_cores = in_cores.reshape(2, rows, depth // 2)
    in_here = jnp.where(core == 0, in_cores[0], in_cores[1])
    in_there = jnp.where(core == 0, in_cores[1], in_cores[0])
    stream = residual.reshape(rows, width).astype(F32)
    shift, scale, gate = modulation[0, 0:1], 1.0 + modulation[0, 1:2], modulation[0, 2:3]
    final32 = final_all.astype(F32)
    scale_final, shift_final = exact_dot(scale, final32), exact_dot(shift, final32)
    down_projected = dot(flat_in, down_all).astype(BF16)
    adapter_term = ADAPTER_SCALE * dot_t(down_projected, up_all)
    final_twice = jnp.concatenate([final_all, final_all], axis=1)

    target_rows = targets.reshape(rows, channels).astype(F32)
    mask_rows = jnp.broadcast_to(repaint_mask.astype(F32)[0], (kinds, tokens)).reshape(rows, 1)

    ready = (in_here, in_there, final_all, final_twice, up_all, down_projected, adapter_term)
    here, ready = lax.optimization_barrier((here, ready))
    in_here, in_there, final_all, final_twice, up_all, down_projected, adapter_term = ready
    there = lax.ppermute(here, "c", SWAP)
    frozen = dot(in_here, here) + dot(in_there, there)
    hidden_ref = stream + gate * frozen
    hidden_pol = hidden_ref + gate * adapter_term

    def head_out(hidden):
        centred = hidden - jnp.mean(hidden, axis=-1, keepdims=True)
        variance = jnp.mean(centred * centred, axis=-1, keepdims=True)
        inverse = lax.rsqrt(variance + NORM_EPS)
        normed = centred * inverse
        return dot((normed * scale + shift).astype(BF16), final_all), normed, inverse

    pred_pol, normed, inverse = head_out(hidden_pol)
    pred_ref, _, _ = head_out(hidden_ref)
    miss_pol = pred_pol - target_rows
    miss_ref = pred_ref - target_rows

    def by_kind(value):
        return jnp.sum(value.reshape(kinds, -1), axis=1)

    errors = jnp.concatenate(
        [by_kind(mask_rows * miss_pol * miss_pol), by_kind(mask_rows * miss_ref * miss_ref)]
    )
    weight_t = (2.0 - timesteps.astype(F32) / 1000.0) / seqs
    errors = jnp.concatenate([errors / normaliser, weight_t])

    signs = jnp.repeat(jnp.array([2.0, -2.0], F32), tokens)[:, None]
    grad_pred = signs * mask_rows * miss_pol
    first = jnp.sum(grad_pred * scale_final, axis=1, keepdims=True) / width
    second = jnp.sum(grad_pred * (pred_pol - shift_final), axis=1, keepdims=True) / width
    grad_norm = dot_t(in_two(grad_pred, 1), final_twice) * scale
    update = (gate * (inverse * (grad_norm - first - normed * second))).astype(BF16)
    up_gradient = ADAPTER_SCALE * t_dot(update, down_projected)
    grad_low = in_two(ADAPTER_SCALE * dot(update, up_all), 1)
    down_gradient = jnp.stack([t_dot(in_here, grad_low), t_dot(in_there, grad_low)])
    down_gradient = down_gradient[:, :, :rank] + down_gradient[:, :, rank:]

    down_gradient = down_gradient.reshape(2, zs, 2, own, rank)
    down_gradient = jnp.where(core == 0, down_gradient, down_gradient[::-1])
    down_gradient = down_gradient.transpose(2, 0, 1, 3, 4)
    up_gradient = up_gradient.reshape(2, zs, 2, 2 * own, rank).transpose(0, 2, 1, 3, 4)
    piece = 3 * own // seqs
    grads = jnp.concatenate([down_gradient, up_gradient], axis=3)
    grads = grads.reshape(2, 2, zs, seqs, piece, rank).transpose(0, 1, 3, 4, 2, 5)
    grads = grads.reshape(4 * seqs, piece * zs, rank).astype(BF16)
    errors = jnp.pad(in_three(errors), ((0, 5), (0, rank - errors.shape[0])))
    errors = jnp.broadcast_to(errors[None], (4 * seqs,) + errors.shape)
    grads = jnp.concatenate([grads, errors], axis=1)
    grads = lax.all_to_all(grads, ("xh", "c") + TOKENS, 0, 0)
    errors = jnp.sum(grads[:, piece * zs : piece * zs + 3].astype(F32), axis=1)
    errors = jnp.sum(errors.reshape(4, seqs, rank), axis=1)
    delta = errors[:, 0:1] - errors[:, 2:3] - (errors[:, 1:2] - errors[:, 3:4])
    weight_t = errors[:, 4:5]
    logits = -DPO_BETA * weight_t * delta
    mine = jnp.arange(4)[:, None] == 2 * xh + core
    pair_loss = jnp.sum(jnp.where(mine, jax.nn.softplus(-logits), 0.0), axis=0)
    slope = jax.nn.sigmoid(-logits) * DPO_BETA * weight_t / normaliser
    grads = grads[:, : piece * zs].astype(F32).reshape(4, seqs, piece, zs, rank)
    grads = jnp.sum(slope[:, :, None, None, None] * grads, axis=(0, 1))
    grads = lax.all_to_all(grads.transpose(1, 0, 2).astype(BF16), "z", 0, 0).astype(F32)
    grads = spread(jnp.sum(grads, axis=0), TOKENS, seqs).reshape(3 * own, rank)
    return (pair_loss, grads[:own], grads[own:])


def solution(mesh):
    seqs = mesh.shape["seq"]
    fsdp = mesh.shape["fsdp"]
    fine = Mesh(mesh.devices.reshape(2, fsdp // 4, 2, 2, seqs // 2), FINE)
    in_specs = (
        P(OWNERS, None, TOKENS, None),
        P(OWNERS, None, TOKENS, None),
        P(OWNERS, None, TOKENS, None),
        P(OWNERS, TOKENS),
        P(OWNERS),
        P(OWNERS, None, None),
        P(OWNERS, None),
        P(OWNERS, None),
        P(OWNERS, None),
        P(OWNERS, None),
    )
    out_specs = (P(OWNERS), P(OWNERS, None), P(OWNERS, None))
    return jax.shard_map(local, mesh=fine, in_specs=in_specs, out_specs=out_specs, check_vma=False)
```

```python
import jax
import jax.numpy as jnp
from jax import lax
from jax.sharding import Mesh
from jax.sharding import PartitionSpec as P

NORM_EPS = 1e-06
DPO_BETA = 10.0
ADAPTER_SCALE = 1.0
FINE = ("xh", "z", "c", "xl", "y")
OWNERS = ("xh", "z", "c")
TOKENS = ("xl", "y")
F32 = jnp.float32
BF16 = jnp.bfloat16
SWAP = [(0, 1), (1, 0)]


def exact_dot(a, b):
    return jnp.dot(a, b, preferred_element_type=F32, precision=lax.Precision.HIGHEST)


def dot(a, b):
    return jnp.dot(a, b, preferred_element_type=F32)


def dot_t(a, b):
    return lax.dot_general(a, b, (((1,), (1,)), ((), ())), preferred_element_type=F32)


def t_dot(a, b):
    return lax.dot_general(a, b, (((0,), (0,)), ((), ())), preferred_element_type=F32)


def in_three(value):
    first = lax.reduce_precision(value, 8, 7)
    rest = value - first
    second = lax.reduce_precision(rest, 8, 7)
    return jnp.stack([first, second, rest - second]).astype(BF16)


def in_two(value, axis):
    first = lax.reduce_precision(value, 8, 7)
    return jnp.concatenate([first, value - first], axis=axis).astype(BF16)


def spread(value, axes, size):
    return lax.all_to_all(jnp.broadcast_to(value[None], (size,) + value.shape), axes, 0, 0)


def gather_small(down, up, last, zs, seqs, xh, core, seq):
    own, rank = down.shape
    channels = last.shape[1]
    packed = jnp.concatenate(
        [down, up, jnp.concatenate([last[:own], last[own:]], axis=1)], axis=0
    )
    piece = 4 * own // seqs
    packed = lax.dynamic_index_in_dim(packed.reshape(seqs, piece, rank), seq, 0, keepdims=False)
    packed = jnp.stack([packed, lax.ppermute(packed, "xh", SWAP)])
    packed = lax.all_gather(packed, "z", axis=0)
    here = spread(packed, TOKENS, seqs)
    there = lax.ppermute(here, "c", SWAP)
    both = jnp.where(core == 0, jnp.stack([here, there]), jnp.stack([there, here]))
    both = jnp.where(xh == 0, both, both[:, :, :, ::-1])
    both = both.transpose(3, 2, 0, 1, 4, 5).reshape(4 * zs, 4 * own, rank)
    down = both[:, :own].reshape(-1, rank)
    up = both[:, own : 3 * own].reshape(-1, rank)
    last = both[:, 3 * own :].reshape(4 * zs, own, 2, channels).transpose(0, 2, 1, 3)
    return down, up, last.reshape(-1, channels)


def local(
    attended,
    residual,
    targets,
    repaint_mask,
    timesteps,
    modulation,
    output_weight,
    adapter_down,
    adapter_up,
    latent_weight,
):
    _, kinds, tokens, depth = attended.shape
    width = residual.shape[-1]
    channels = targets.shape[-1]
    rank = adapter_down.shape[1]
    rows = kinds * tokens
    own = output_weight.shape[0]
    zs, ys = lax.axis_size("z"), lax.axis_size("y")
    seqs = 2 * ys
    xh, core = lax.axis_index("xh"), lax.axis_index("c")
    normaliser = float(tokens * seqs * channels)

    pair = lax.all_gather(output_weight, ("xh", "xl"), axis=0, axis_index_groups=[[0, 3], [1, 2]])
    here = lax.all_gather(pair, "z", axis=0).reshape(depth // 2, width)

    down_all, up_all, final_all = gather_small(
        adapter_down, adapter_up, latent_weight, zs, seqs, xh, core, lax.axis_index(TOKENS)
    )
    flat_in = attended.reshape(rows, depth)
    in_cores = flat_in.reshape(rows, 2, zs, 2, own).transpose(3, 0, 2, 1, 4)
    in_cores = in_cores.reshape(2, rows, depth // 2)
    in_here = jnp.where(core == 0, in_cores[0], in_cores[1])
    in_there = jnp.where(core == 0, in_cores[1], in_cores[0])
    in_away = lax.ppermute(in_there, "c", SWAP)
    stream = residual.reshape(rows, width).astype(F32)
    shift, scale, gate = modulation[0, 0:1], 1.0 + modulation[0, 1:2], modulation[0, 2:3]
    final32 = final_all.astype(F32)
    scale_final, shift_final = exact_dot(scale, final32), exact_dot(shift, final32)
    down_projected = dot(flat_in, down_all).astype(BF16)
    adapter_term = ADAPTER_SCALE * dot_t(down_projected, up_all)
    final_twice = jnp.concatenate([final_all, final_all], axis=1)

    target_rows = targets.reshape(rows, channels).astype(F32)
    mask_rows = jnp.broadcast_to(repaint_mask.astype(F32)[0], (kinds, tokens)).reshape(rows, 1)

    ready = (in_here, in_there, in_away, final_all, final_twice, up_all)
    ready = ready + (down_projected, adapter_term)
    here, ready = lax.optimization_barrier((here, ready))
    in_here, in_there, in_away, final_all, final_twice, up_all = ready[:6]
    down_projected, adapter_term = ready[6:]
    away = lax.ppermute(dot(in_away, here).astype(BF16), "c", SWAP)
    frozen = dot(in_here, here) + away.astype(F32)
    hidden_ref = stream + gate * frozen
    hidden_pol = hidden_ref + gate * adapter_term

    def head_out(hidden):
        centred = hidden - jnp.mean(hidden, axis=-1, keepdims=True)
        variance = jnp.mean(centred * centred, axis=-1, keepdims=True)
        inverse = lax.rsqrt(variance + NORM_EPS)
        normed = centred * inverse
        return dot((normed * scale + shift).astype(BF16), final_all), normed, inverse

    pred_pol, normed, inverse = head_out(hidden_pol)
    pred_ref, _, _ = head_out(hidden_ref)
    miss_pol = pred_pol - target_rows
    miss_ref = pred_ref - target_rows

    def by_kind(value):
        return jnp.sum(value.reshape(kinds, -1), axis=1)

    errors = jnp.concatenate(
        [by_kind(mask_rows * miss_pol * miss_pol), by_kind(mask_rows * miss_ref * miss_ref)]
    )
    weight_t = (2.0 - timesteps.astype(F32) / 1000.0) / seqs
    errors = jnp.concatenate([errors / normaliser, weight_t])

    signs = jnp.repeat(jnp.array([2.0, -2.0], F32), tokens)[:, None]
    grad_pred = signs * mask_rows * miss_pol
    first = jnp.sum(grad_pred * scale_final, axis=1, keepdims=True) / width
    second = jnp.sum(grad_pred * (pred_pol - shift_final), axis=1, keepdims=True) / width
    grad_norm = dot_t(in_two(grad_pred, 1), final_twice) * scale
    update = (gate * (inverse * (grad_norm - first - normed * second))).astype(BF16)
    up_gradient = ADAPTER_SCALE * t_dot(update, down_projected)
    grad_low = in_two(ADAPTER_SCALE * dot(update, up_all), 1)
    down_gradient = jnp.stack([t_dot(in_here, grad_low), t_dot(in_there, grad_low)])
    down_gradient = down_gradient[:, :, :rank] + down_gradient[:, :, rank:]

    down_gradient = down_gradient.reshape(2, zs, 2, own, rank)
    down_gradient = jnp.where(core == 0, down_gradient, down_gradient[::-1])
    down_gradient = down_gradient.transpose(2, 0, 1, 3, 4)
    up_gradient = up_gradient.reshape(2, zs, 2, 2 * own, rank).transpose(0, 2, 1, 3, 4)
    piece = 3 * own // seqs
    grads = jnp.concatenate([down_gradient, up_gradient], axis=3)
    grads = grads.reshape(2, 2, zs, seqs, piece, rank).transpose(0, 1, 3, 4, 2, 5)
    grads = grads.reshape(4 * seqs, piece * zs, rank).astype(BF16)
    errors = jnp.pad(in_three(errors), ((0, 5), (0, rank - errors.shape[0])))
    errors = jnp.broadcast_to(errors[None], (4 * seqs,) + errors.shape)
    grads = jnp.concatenate([grads, errors], axis=1)
    grads = lax.all_to_all(grads, ("xh", "c") + TOKENS, 0, 0)
    errors = jnp.sum(grads[:, piece * zs : piece * zs + 3].astype(F32), axis=1)
    errors = jnp.sum(errors.reshape(4, seqs, rank), axis=1)
    delta = errors[:, 0:1] - errors[:, 2:3] - (errors[:, 1:2] - errors[:, 3:4])
    weight_t = errors[:, 4:5]
    logits = -DPO_BETA * weight_t * delta
    mine = jnp.arange(4)[:, None] == 2 * xh + core
    pair_loss = jnp.sum(jnp.where(mine, jax.nn.softplus(-logits), 0.0), axis=0)
    slope = jax.nn.sigmoid(-logits) * DPO_BETA * weight_t / normaliser
    grads = grads[:, : piece * zs].astype(F32).reshape(4, seqs, piece, zs, rank)
    grads = jnp.sum(slope[:, :, None, None, None] * grads, axis=(0, 1))
    grads = lax.all_to_all(grads.transpose(1, 0, 2).astype(BF16), "z", 0, 0).astype(F32)
    grads = spread(jnp.sum(grads, axis=0), TOKENS, seqs).reshape(3 * own, rank)
    return (pair_loss, grads[:own], grads[own:])


def solution(mesh):
    seqs = mesh.shape["seq"]
    fsdp = mesh.shape["fsdp"]
    fine = Mesh(mesh.devices.reshape(2, fsdp // 4, 2, 2, seqs // 2), FINE)
    in_specs = (
        P(OWNERS, None, TOKENS, None),
        P(OWNERS, None, TOKENS, None),
        P(OWNERS, None, TOKENS, None),
        P(OWNERS, TOKENS),
        P(OWNERS),
        P(OWNERS, None, None),
        P(OWNERS, None),
        P(OWNERS, None),
        P(OWNERS, None),
        P(OWNERS, None),
    )
    out_specs = (P(OWNERS), P(OWNERS, None), P(OWNERS, None))
    return jax.shard_map(local, mesh=fine, in_specs=in_specs, out_specs=out_specs, check_vma=False)
```
